32 devices in a mesh: dp: 4 (over x, core), expert: 8 (over z, y).
Axes of the slice: x: 2, y: 2, z: 4, core: 2. Of those that a mesh axis runs over, the one named last changes fastest.
Arguments:
- tokens: bfloat16 [4096, 768], P(('dp', 'expert')), may hold values from -6 to 6
- segment_ids: int32 [32, 128], P(('dp', 'expert')), may hold values from 0 to 1, never falling along the last dimension, each value on 1 to 96 neighbouring positions
- routes: int32 [4096, 1], P(('dp', 'expert')), may hold values from 0 to 7; in each aligned block of 128 rows (0 to 127, 128 to 255, ...) at most 20 rows name the same one
- bucket_table: int32 [255], replicated, may hold values from 0 to 31
- gain_attn: bfloat16 [768], P(('dp', 'expert')), may hold values from 0.5 to 1.5
- w_query: bfloat16 [768, 768], P(('dp', 'expert')), may hold values from -0.0546875 to 0.0546875
- w_key: bfloat16 [768, 768], P(('dp', 'expert')), may hold values from -0.21875 to 0.21875
- w_value: bfloat16 [768, 768], P(('dp', 'expert')), may hold values from -0.21875 to 0.21875
- w_output: bfloat16 [768, 768], P(('dp', 'expert')), may hold values from -0.875 to 0.875
- rel_bias: float32 [32, 12], replicated, may hold values from -3 to 3
- gain_ffn: bfloat16 [768], P(('dp', 'expert')), may hold values from 0.5 to 1.5
- w_router: bfloat16 [768, 8], P(('dp', 'expert')), may hold values from -0.109375 to 0.109375
- w_in: bfloat16 [8, 768, 3072], P('expert'), may hold values from -0.21875 to 0.21875
- w_out: bfloat16 [8, 3072, 768], P('expert'), may hold values from -4 to 4
- cotangent: bfloat16 [4096, 768], P(('dp', 'expert')), may hold values from -6 to 6
Outputs:
- output: bfloat16 [4096, 768], P(('dp', 'expert'))
- grad_tokens: bfloat16 [4096, 768], P(('dp', 'expert'))
- grad_gain_attn: float32 [768], P(('dp', 'expert'))
- grad_w_query: float32 [768, 768], P(('dp', 'expert'))
- grad_w_key: float32 [768, 768], P(('dp', 'expert'))
- grad_w_value: float32 [768, 768], P(('dp', 'expert'))
- grad_w_output: float32 [768, 768], P(('dp', 'expert'))
- grad_rel_bias: float32 [32, 12], replicated
- grad_gain_ffn: float32 [768], P(('dp', 'expert'))
- grad_w_router: float32 [768, 8], P(('dp', 'expert'))
- grad_w_in: float32 [8, 768, 3072], P('expert', None, 'dp')
- grad_w_out: float32 [8, 3072, 768], P('expert', 'dp')
The draws below stay inside these ranges and needn't reach their ends.
Inputs may be any that keep to these rules, and one draw needn't show every extreme that they name: `routes`: in the rows of one device no expert is named more than 20 times. `segment_ids`: along a sequence the numbers never fall; a document holds 1 to 96 tokens.
All inputs are finite; a program needn't handle non-finite values.
Results may differ from the reference program's by a relative error of at most 0.018.
Values may be sent and summed in bfloat16 or wider, within the bound.
A program may use at most 128 MiB of HBM per device.

```python
import math
import jax
import jax.numpy as jnp
import numpy as np
from jax import lax

D = 768
HEADS = 12
HEAD_DIM = 64
FF = 3072
BUCKETS = 32
TOK_DEV = 128
EXPERTS = 8
CAP = 20
SEQS = 32
TOKENS = 4096
SEG_COUNT = 2
SEG_MOST = 96
OFFSETS = 255


def touch_ends(result, own_key, smallest, largest):
    longest = result.shape.index(max(result.shape))
    spots = []
    for shift in (0, 1):
        where = [jax.random.randint(jax.random.fold_in(own_key, axis), (), 0, length) for axis, length in enumerate(result.shape)]
        where[longest] = (where[longest] + shift) % result.shape[longest]
        spots.append(tuple(where))
    return result.at[spots[0]].set(smallest).at[spots[1]].set(largest)


def shard_levels(key, extent, split, least, largest):
    def one(axis_at, shards_of):
        heights = jax.random.uniform(jax.random.fold_in(jax.random.fold_in(key, 6), axis_at), (shards_of,), jnp.float32, least / len(split), largest / len(split))
        return jnp.repeat(jnp.exp(heights), extent[axis_at] // shards_of).reshape((-1,) + (1,) * (len(extent) - axis_at - 1))

    level = one(*split[0])
    for cut in split[1:]:
        level = level * one(*cut)
    return level


def profile(amount, total, most, slope):
    loads = [(1 << 20) // math.isqrt(rank ** slope) + 1 for rank in range(2, amount + 1)]
    spare, counts = total - most - (amount - 1), [1] * (amount - 1)
    while spare > 0:
        free = [i for i in range(amount - 1) if counts[i] < most]
        pool, left = sum([loads[i] for i in free]), spare
        for i in free:
            addition = min(most - counts[i], max(1, left * loads[i] // pool), spare)
            counts[i] = counts[i] + addition
            spare = spare - addition
    return np.array([most] + counts)


def ragged(stream_key, amount, total, bound, lean):
    if amount == 2:
        one = jax.random.randint(stream_key, (), max(1, total - bound), min(bound, total - 1) + 1)
        return jnp.stack([one, total - one])
    sizes = jnp.asarray(profile(amount, total, bound, lean), jnp.int32)
    twos = (amount - 1) // 2
    source_of, sink = sizes[1:1 + 2 * twos:2], sizes[2:2 + 2 * twos:2]
    room = jnp.minimum(source_of - 1, bound - sink)
    passed = jax.random.randint(jax.random.fold_in(stream_key, 1), (twos,), 0, 1 << 20) % (room + 1)
    sizes = sizes.at[1:1 + 2 * twos:2].set(source_of - passed).at[2:2 + 2 * twos:2].set(sink + passed)
    return sizes[jax.random.permutation(jax.random.fold_in(stream_key, 2), amount)]


def deal_out(key, own, number, rows, amount, top, most, slope):
    sequence = jax.random.permutation(key, amount)
    crowded, ordinary = portions_of(amount, rows * top, most, slope, True), portions_of(amount, rows * top, most, slope, False)
    places = jnp.arange(amount)

    def named(sizes, turn):
        used = int((sizes > 0).sum())
        fixed = max(1, used // 4)
        passed = fixed + (places - fixed + turn * (used - fixed)) % max(1, amount - fixed)
        return jnp.zeros((amount,), jnp.int32).at[sequence[jnp.where(places < fixed, places, passed)]].set(jnp.asarray(sizes, jnp.int32))

    sizes = jnp.where(number % 4 == 0, named(crowded, number // 4), named(ordinary, number - number // 4 - 1))
    mixed = jax.random.permutation(jax.random.fold_in(own, 3), amount)
    donor, sink = mixed[0:amount // 2 * 2:2], mixed[1:amount // 2 * 2:2]
    room = jnp.minimum(sizes[donor] - 1, most - sizes[sink]) // 2
    room = jnp.where((donor == sequence[0]) | (sink == sequence[0]) | (sizes[sink] == 0), 0, jnp.maximum(room, 0))
    passed = jax.random.randint(jax.random.fold_in(own, 4), (amount // 2,), 0, 1 << 20) % (room + 1)
    sizes = sizes.at[donor].add(-passed).at[sink].add(passed)
    items = jnp.searchsorted(jnp.cumsum(sizes), jnp.arange(rows * top), side="right").astype(jnp.int32)
    table = items.reshape(top, rows).T
    table = table[jax.random.permutation(jax.random.fold_in(own, 1), rows)]
    turn = jax.random.randint(jax.random.fold_in(own, 2), (rows, 1), 0, top)
    return jnp.take_along_axis(table, (jnp.arange(top)[None, :] + turn) % top, axis=1)


def portions_of(amount, total, most, skew, full):
    portions = [(1 << 20) // math.isqrt(standing ** skew) + 1 for standing in range(1, amount + 1)]
    largest = most if full else min(most, max(-(-total // amount), total * portions[0] // sum(portions)))
    least = 1 if total - largest >= amount - 1 else 0
    holding, surplus = [largest] + [least] * (amount - 1), total - largest - least * (amount - 1)
    while surplus > 0:
        movable = [i for i in range(1, amount) if holding[i] < largest] or [i for i in range(1, amount) if holding[i] < most]
        mass, remaining = sum([portions[i] for i in movable]), surplus
        for i in movable:
            addition = min(most - holding[i], max(1, remaining * portions[i] // mass), surplus)
            holding[i] = holding[i] + addition
            surplus = surplus - addition
    return np.array(holding)


def noise(own_key, dims, deviation, limit, cuts=(), held_as=jnp.bfloat16):
    gain = shard_levels(own_key, dims, cuts, -0.22, 0.18) if cuts else 1.0
    entries = jax.random.normal(own_key, dims, jnp.float32) * deviation * gain
    return jnp.minimum(jnp.maximum(entries, -limit), limit).astype(held_as)


def setup_inputs(seed: int = 0) -> dict:
    key_list = jax.random.split(jax.random.key(seed), 16)
    tokens = noise(key_list[0], (TOKENS, D), 1.0, 6.0, ((0, 32),))
    segment_ids = jax.vmap(lambda own: jnp.searchsorted(jnp.cumsum(ragged(own, SEG_COUNT, TOK_DEV, SEG_MOST, 1)), jnp.arange(TOK_DEV), side="right"))(jax.random.split(key_list[1], SEQS)).reshape((SEQS, TOK_DEV)).astype(jnp.int32)
    routes_keys = jax.random.split(jax.random.fold_in(key_list[2], 1), TOKENS // TOK_DEV)
    routes_turns = jax.random.permutation(jax.random.fold_in(key_list[2], 3), TOKENS // TOK_DEV)
    routes = jax.vmap(lambda own, number: deal_out(jax.random.fold_in(key_list[2], 2), own, number, TOK_DEV, EXPERTS, 1, CAP, 2))(routes_keys, routes_turns).reshape((TOKENS, 1))
    bucket_table = touch_ends(jax.random.randint(key_list[3], (OFFSETS,), 0, BUCKETS), jax.random.fold_in(key_list[3], 1), 0, BUCKETS - 1).astype(jnp.int32)
    gain_attn = jnp.clip(1.0 + 0.1 * jax.random.normal(key_list[4], (D,), jnp.float32), 0.5, 1.5).astype(jnp.bfloat16)
    w_query = noise(key_list[5], (D, D), (16 * D) ** -0.5, 0.0546875, ((0, 32),))
    w_key = noise(key_list[6], (D, D), D ** -0.5, 0.21875, ((0, 32),))
    w_value = noise(key_list[7], (D, D), D ** -0.5, 0.21875, ((0, 32),))
    w_output = noise(key_list[8], (D, D), (D // 16) ** -0.5, 0.875, ((0, 32),))
    rel_bias = noise(key_list[9], (BUCKETS, HEADS), 0.5, 3.0, (), jnp.float32)
    gain_ffn = jnp.clip(1.0 + 0.1 * jax.random.normal(key_list[10], (D,), jnp.float32), 0.5, 1.5).astype(jnp.bfloat16)
    w_router = noise(key_list[11], (D, EXPERTS), (4 * D) ** -0.5, 0.109375, ((0, 32),))
    w_in = noise(key_list[12], (EXPERTS, D, FF), D ** -0.5, 0.21875, ((0, 8),))
    w_out = noise(key_list[13], (EXPERTS, FF, D), (max(1, FF // 1536)) ** -0.5, 4.0, ((0, 8),))
    cotangent = noise(key_list[14], (TOKENS, D), 1.0, 6.0, ((0, 32),))
    return dict(tokens=tokens, segment_ids=segment_ids, routes=routes, bucket_table=bucket_table, gain_attn=gain_attn, w_query=w_query, w_key=w_key, w_value=w_value, w_output=w_output, rel_bias=rel_bias, gain_ffn=gain_ffn, w_router=w_router, w_in=w_in, w_out=w_out, cotangent=cotangent)


@jax.custom_vjp
def low(v):
    return lax.optimization_barrier(v.astype(jnp.bfloat16)).astype(jnp.float32)

@jax.custom_vjp
def low_back(v):
    return v

def low_keep(v):
    return (low(v), None)

def low_pass(kept, grad):
    return (grad,)

def back_keep(v):
    return (v, None)

def back_low(kept, grad):
    return (low(grad),)
low.defvjp(low_keep, low_pass)
low_back.defvjp(back_keep, back_low)
epsilon = 1e-06
highest = lax.Precision.HIGHEST

def round_both(values):
    return low_back(low(values))

def rms_scale(values):
    return lax.rsqrt(lax.optimization_barrier(jnp.mean(values * values, axis=-1, keepdims=True)) + epsilon)

def gelu_tanh(values):
    return jax.nn.gelu(values, approximate=True)

def bias_table(rel_bias, bucket_table):
    offsets = bucket_table.shape[0]
    length = (offsets + 1) // 2
    onehot = (bucket_table[:, None] == jnp.arange(rel_bias.shape[0], dtype=jnp.int32)[None, :]).astype(jnp.float32)
    per_offset = jnp.dot(onehot, rel_bias, precision=highest).T
    padded = jnp.concatenate([per_offset, jnp.zeros((per_offset.shape[0], 1), jnp.float32)], axis=1)
    repeated = jnp.tile(padded, (1, length))[:, :length * offsets]
    return repeated.reshape(per_offset.shape[0], length, offsets)[:, :, length - 1:offsets]

def encoder_layer(hidden_in, gain_attn, w_query, w_key, w_value, w_output, rel_bias, gain_ffn, w_router, w_in, w_out, segment_ids, routes, bucket_table):
    normed = low(hidden_in * rms_scale(hidden_in) * gain_attn)
    query = round_both(jnp.dot(normed, w_query, precision=highest))
    keyed = round_both(jnp.dot(normed, w_key, precision=highest))
    valued = round_both(jnp.dot(normed, w_value, precision=highest))
    pos_bias = bias_table(rel_bias, bucket_table)
    group_size = math.gcd(SEQS, 16)
    blocks = SEQS // group_size
    split_shape = (blocks, group_size, TOK_DEV, HEADS, HEAD_DIM)

    def attend(members):
        query_part, key_part, value_part, segment = members
        scores = jnp.einsum('gqhe,gkhe->ghqk', query_part, key_part, precision=highest)
        scores = low_back(scores) + pos_bias[None]
        same_doc = segment[:, None, :, None] == segment[:, None, None, :]
        scores = jnp.where(same_doc, scores, -1e+30)
        attn_probs = jax.nn.softmax(scores, axis=-1)
        return jnp.einsum('ghqk,gkhe->gqhe', low(attn_probs), value_part, precision=highest)
    attended = lax.map(jax.checkpoint(attend), (query.reshape(split_shape), keyed.reshape(split_shape), valued.reshape(split_shape), segment_ids.reshape(blocks, group_size, TOK_DEV)))
    attended = round_both(attended.reshape(SEQS * TOK_DEV, D))
    residual = hidden_in + low_back(jnp.dot(attended, w_output, precision=highest))
    normed_two = low(residual * rms_scale(residual) * gain_ffn)
    logits = jnp.dot(normed_two, w_router, precision=highest)
    router_probs = jax.nn.softmax(logits, axis=-1)
    choose = (routes[:, 0:1] == jnp.arange(EXPERTS, dtype=jnp.int32)[None, :]).astype(jnp.int32)
    gate_prob = lax.optimization_barrier(jnp.sum(router_probs * choose.astype(jnp.float32), axis=-1))
    grouped = choose.reshape(SEQS, TOK_DEV, EXPERTS)
    earlier = (jnp.cumsum(grouped, axis=1) - grouped).astype(jnp.int32)
    position = lax.optimization_barrier(jnp.sum(earlier * grouped, axis=-1)).astype(jnp.int32) + routes[:, 0].reshape(SEQS, TOK_DEV) * CAP
    dispatch = (position[:, :, None] == jnp.arange(EXPERTS * CAP, dtype=jnp.int32)[None, None, :]).astype(jnp.float32)
    expert_rows = low_back(normed_two).reshape(SEQS, TOK_DEV, D)
    outgoing = jnp.einsum('stc,std->scd', dispatch, expert_rows, precision=highest)
    outgoing = outgoing.reshape(SEQS, EXPERTS, CAP, D).transpose(1, 0, 2, 3).reshape(EXPERTS, SEQS * CAP, D)

    def expert_ffn(members):
        slot_rows, first_w, second_w = members
        pre_act = low_back(jnp.dot(slot_rows, first_w, precision=highest))
        hidden_act = low(gelu_tanh(pre_act))
        return round_both(jnp.dot(hidden_act, second_w, precision=highest))
    returned = lax.map(jax.checkpoint(expert_ffn), (outgoing, w_in, w_out))
    returned = returned.reshape(EXPERTS, SEQS, CAP, D).transpose(1, 0, 2, 3).reshape(SEQS, EXPERTS * CAP, D)
    combined = jnp.einsum('stc,scd->std', dispatch, returned, precision=highest).reshape(SEQS * TOK_DEV, D)
    return residual + gate_prob[:, None] * combined

def reference(tokens, segment_ids, routes, bucket_table, gain_attn, w_query, w_key, w_value, w_output, rel_bias, gain_ffn, w_router, w_in, w_out, cotangent):
    floats = tuple((member.astype(jnp.float32) for member in (tokens, gain_attn, w_query, w_key, w_value, w_output, rel_bias, gain_ffn, w_router, w_in, w_out)))

    def forward(hidden_in, gain_one, query_w, key_w, value_w, output_w, table_bias, gain_two, router_w, first_w, second_w):
        return encoder_layer(hidden_in, gain_one, query_w, key_w, value_w, output_w, table_bias, gain_two, router_w, first_w, second_w, segment_ids, routes, bucket_table)
    output, pullback = jax.vjp(forward, *floats)
    grads = pullback(cotangent.astype(jnp.float32))
    return (output.astype(jnp.bfloat16), grads[0].astype(jnp.bfloat16), grads[1], grads[2], grads[3], grads[4], grads[5], grads[6], grads[7], grads[8], grads[9], grads[10])
```

```python
import functools

import jax
import jax.numpy as jnp
from jax import lax
from jax.experimental import pallas as pl
from jax.experimental.pallas import tpu as pltpu
from jax.sharding import PartitionSpec as P

epsilon = 1e-06
highest = lax.Precision.HIGHEST


def gelu_tanh(values):
    return jax.nn.gelu(values, approximate=True)


def bias_table(rel_bias, bucket_table):
    offsets = bucket_table.shape[0]
    length = (offsets + 1) // 2
    onehot = (
        bucket_table[:, None] == jnp.arange(rel_bias.shape[0], dtype=jnp.int32)[None, :]
    ).astype(jnp.float32)
    per_offset = jnp.dot(onehot, rel_bias, precision=highest).T
    padded = jnp.concatenate([per_offset, jnp.zeros((per_offset.shape[0], 1), jnp.float32)], axis=1)
    repeated = jnp.tile(padded, (1, length))[:, : length * offsets]
    return repeated.reshape(per_offset.shape[0], length, offsets)[:, :, length - 1 : offsets]


def norm_back(grad_normed, unit, scale, gain):
    grad_unit = grad_normed * gain
    grad_gain = jnp.sum(grad_normed * unit, axis=0)
    grad_input = scale * (grad_unit - unit * jnp.mean(grad_unit * unit, axis=-1, keepdims=True))
    return (grad_gain, grad_input)


def doubling(count):
    return [2**step for step in range(count.bit_length() - 1)]


def exchange_orders(dp_size, expert_size):
    x_size = dp_size // 2
    y_size = min(x_size, expert_size)
    z_size = expert_size // y_size
    along_y = doubling(y_size)
    along_z = [y_size * step for step in doubling(z_size)]
    cores = [expert_size]
    along_x = [2 * expert_size * step for step in doubling(x_size)]
    return (along_z + along_y + along_x + cores, along_z + along_x + along_y + cores)


def signed(me, weight):
    return weight * (1 - 2 * ((me // weight) % 2))


def member(me, order, slot):
    other = me
    for step, weight in enumerate(order):
        other = other + ((slot // 2**step) % 2) * signed(me, weight)
    return other


def device_of(index, expert_size):
    return (index // expert_size, index % expert_size)


def meet(me, weights, expert_size):
    barrier = pltpu.get_barrier_semaphore()
    for weight in weights:
        pl.semaphore_signal(
            barrier,
            inc=1,
            device_id=device_of(me + signed(me, weight), expert_size),
            device_id_type=pl.DeviceIdType.MESH,
        )
    pl.semaphore_wait(barrier, len(weights))


def send(me, weight, expert_size, source, target, send_sem, recv_sem):
    copy = pltpu.make_async_remote_copy(
        src_ref=source,
        dst_ref=target,
        send_sem=send_sem,
        recv_sem=recv_sem,
        device_id=device_of(me + signed(me, weight), expert_size),
        device_id_type=pl.DeviceIdType.MESH,
    )
    copy.start()
    return copy


def gather_kernel(orders, expert_size, *refs):
    shards, outs, held, sems = refs[:2], refs[2:4], refs[4:6], refs[6:]
    send_sem, recv_sem = sems
    me = lax.axis_index("dp") * expert_size + lax.axis_index("expert")
    stages = len(orders[0])
    for shard, buffer in zip(shards, held):
        buffer[0] = shard[...]
    meet(me, orders[0], expert_size)
    copies = [[], []]
    for stage in range(stages):
        size = 2**stage
        for part in range(2):
            if stage:
                copies[part][-1].wait_recv()
            copies[part].append(
                send(
                    me,
                    orders[part][stage],
                    expert_size,
                    held[part].at[pl.ds(0, size)],
                    held[part].at[pl.ds(size, size)],
                    send_sem.at[part, stage],
                    recv_sem.at[part, stage],
                )
            )

    def place(part, first, last):
        def body(slot, carry):
            outs[part][member(me, orders[part], slot)] = held[part][slot]
            return carry

        lax.fori_loop(first, last, body, 0)

    half = 2 ** (stages - 1)
    for part in range(2):
        place(part, 0, half)
    for part in range(2):
        copies[part][-1].wait_recv()
        place(part, half, 2 * half)
    for part in range(2):
        for copy in copies[part]:
            copy.wait_send()


def gather_shards(shards, dp_size, expert_size):
    count = dp_size * expert_size
    orders = exchange_orders(dp_size, expert_size)
    stages = len(orders[0])
    shapes = [(count,) + shard.shape for shard in shards]
    vmem = pl.BlockSpec(memory_space=pltpu.VMEM)
    return pl.pallas_call(
        functools.partial(gather_kernel, orders, expert_size),
        out_shape=[jax.ShapeDtypeStruct(shape, jnp.bfloat16) for shape in shapes],
        in_specs=[vmem] * 2,
        out_specs=[vmem] * 2,
        scratch_shapes=[pltpu.VMEM(shape, jnp.bfloat16) for shape in shapes]
        + [pltpu.SemaphoreType.DMA((2, stages)), pltpu.SemaphoreType.DMA((2, stages))],
        compiler_params=pltpu.CompilerParams(
            collective_id=0, has_side_effects=True, vmem_limit_bytes=40 * 2**20
        ),
    )(*shards)


def scatter_kernel(orders, expert_size, *refs):
    grads, small, outs, small_out = refs[:2], refs[2], refs[3:5], refs[5]
    held, landed, small_held, small_landed = refs[6:8], refs[8:10], refs[10], refs[11]
    send_sem, recv_sem = refs[12:]
    me = lax.axis_index("dp") * expert_size + lax.axis_index("expert")
    stages = len(orders[0])
    count = 2**stages
    half = count // 2

    def fill(part, first, last):
        def body(slot, carry):
            held[part][slot] = grads[part][member(me, orders[part], slot)]
            return carry

        lax.fori_loop(first, last, body, 0)

    def start(part, stage):
        size = 2**stage
        return send(
            me,
            orders[part][stage],
            expert_size,
            held[part].at[pl.ds(size, size)],
            landed[part].at[pl.ds(size, size)],
            send_sem.at[part, stage],
            recv_sem.at[part, stage],
        )

    def start_small(stage):
        return send(
            me,
            orders[0][stage],
            expert_size,
            small_held.at[stage],
            small_landed.at[stage],
            send_sem.at[2, stage],
            recv_sem.at[2, stage],
        )

    small_held[stages - 1] = small[...]
    fill(0, half, count)
    meet(me, orders[0], expert_size)
    started = [start(0, stages - 1)]
    fill(1, half, count)
    started.append(start(1, stages - 1))
    small_copy = start_small(stages - 1)
    fill(0, 0, half)
    fill(1, 0, half)
    sent = []
    current = list(started)
    for stage in reversed(range(stages)):
        size = 2**stage
        for part in range(2):
            current[part].wait_recv()
            sent.append(current[part])
            if stage:

                def body(slot, carry):
                    held[part][slot] = (
                        held[part][slot].astype(jnp.float32)
                        + landed[part][slot + size].astype(jnp.float32)
                    ).astype(jnp.bfloat16)
                    return carry

                lax.fori_loop(size // 2, size, body, 0)
                current[part] = start(part, stage - 1)
                lax.fori_loop(0, size // 2, body, 0)
            else:
                outs[part][...] = held[part][0].astype(jnp.float32) + landed[part][1].astype(
                    jnp.float32
                )
        small_copy.wait_recv()
        sent.append(small_copy)
        total = small_held[stage] + small_landed[stage]
        if stage:
            small_held[stage - 1] = total
            small_copy = start_small(stage - 1)
        else:
            small_out[...] = total
    for copy in sent:
        copy.wait_send()


def scatter_sums(grads, small, dp_size, expert_size):
    orders = exchange_orders(dp_size, expert_size)
    stages = len(orders[0])
    shapes = [grad.shape for grad in grads]
    vmem = pl.BlockSpec(memory_space=pltpu.VMEM)
    buffers = [pltpu.VMEM(shape, jnp.bfloat16) for shape in shapes]
    small_buffer = pltpu.VMEM((stages,) + small.shape, jnp.float32)
    return pl.pallas_call(
        functools.partial(scatter_kernel, orders, expert_size),
        out_shape=[jax.ShapeDtypeStruct(shape[1:], jnp.float32) for shape in shapes]
        + [jax.ShapeDtypeStruct(small.shape, jnp.float32)],
        in_specs=[vmem] * 3,
        out_specs=[vmem] * 3,
        scratch_shapes=buffers
        + buffers
        + [small_buffer] * 2
        + [pltpu.SemaphoreType.DMA((3, stages)), pltpu.SemaphoreType.DMA((3, stages))],
        compiler_params=pltpu.CompilerParams(
            collective_id=1, has_side_effects=True, vmem_limit_bytes=40 * 2**20
        ),
    )(*grads, small)


def padded_width(width, rows):
    unit = 128 if rows % 8 == 0 else 2048
    return -(-width // unit) * unit


def block_shape(rows, width):
    return (rows, width) if rows % 8 == 0 else (16, rows * width // 16)


def widen(array, width):
    return jnp.pad(array, ((0, 0), (0, width - array.shape[1])))


def per_device(
    tokens,
    segment_ids,
    routes,
    bucket_table,
    gain_attn,
    w_query,
    w_key,
    w_value,
    w_output,
    rel_bias,
    gain_ffn,
    w_router,
    w_in,
    w_out,
    cotangent,
):
    length, features = tokens.shape
    num_heads = rel_bias.shape[1]
    head_size = features // num_heads
    local_experts = w_in.shape[0]
    owners = lax.axis_size("expert")
    experts = local_experts * owners
    capacity = 5 * length // (4 * experts)
    dp_size = lax.axis_size("dp")
    rows = w_query.shape[0]
    extras = experts + 2
    width_one = padded_width(2 * features + extras, rows)
    width_two = padded_width(2 * features, rows)
    shard_one = widen(
        jnp.concatenate(
            [w_query, w_key, w_router, gain_attn[:, None], gain_ffn[:, None]], axis=1
        ),
        width_one,
    )
    shard_two = widen(jnp.concatenate([w_value, w_output], axis=1), width_two)
    whole_one, whole_two = gather_shards(
        (
            shard_one.reshape(block_shape(rows, width_one)),
            shard_two.reshape(block_shape(rows, width_two)),
        ),
        dp_size,
        owners,
    )
    whole_one = whole_one.reshape(features, width_one)
    whole_two = whole_two.reshape(features, width_two)
    query_w = whole_one[:, :features]
    key_w = whole_one[:, features : 2 * features]
    value_w = whole_two[:, :features]
    output_w = whole_two[:, features : 2 * features]
    router_w = whole_one[:, 2 * features : 2 * features + experts]
    gain_one = whole_one[:, 2 * features + experts]
    gain_two = whole_one[:, 2 * features + experts + 1]
    inputs = tokens.astype(jnp.float32)
    scale_one = lax.rsqrt(jnp.mean(inputs * inputs, axis=-1, keepdims=True) + epsilon)
    unit_one = inputs * scale_one
    normed = (unit_one * gain_one.astype(jnp.float32)).astype(jnp.bfloat16)
    query = (
        jnp.dot(normed, query_w, preferred_element_type=jnp.float32)
        .astype(jnp.bfloat16)
        .reshape(length, num_heads, head_size)
    )
    keyed = (
        jnp.dot(normed, key_w, preferred_element_type=jnp.float32)
        .astype(jnp.bfloat16)
        .reshape(length, num_heads, head_size)
    )
    valued = (
        jnp.dot(normed, value_w, preferred_element_type=jnp.float32)
        .astype(jnp.bfloat16)
        .reshape(length, num_heads, head_size)
    )
    pos_bias = bias_table(rel_bias, bucket_table)
    segment = segment_ids[0]
    same_doc = segment[:, None] == segment[None, :]

    def scores_of():
        raw_scores = jnp.einsum("qhe,khe->hqk", query, keyed, preferred_element_type=jnp.float32)
        return jnp.where(same_doc[None], raw_scores + pos_bias, -1e30)

    scores = scores_of()
    row_peak = jnp.max(scores, axis=-1, keepdims=True)
    exp_scores = jnp.exp(scores - row_peak)
    row_total = jnp.sum(exp_scores, axis=-1, keepdims=True)
    attn_probs = exp_scores / row_total
    log_total = row_peak + jnp.log(row_total)
    attended = jnp.einsum(
        "hqk,khe->qhe", attn_probs.astype(jnp.bfloat16), valued, preferred_element_type=jnp.float32
    )
    attended = attended.astype(jnp.bfloat16).reshape(length, features)
    residual = inputs + jnp.dot(attended, output_w, preferred_element_type=jnp.float32)
    scale_two = lax.rsqrt(jnp.mean(residual * residual, axis=-1, keepdims=True) + epsilon)
    unit_two = residual * scale_two
    normed_two = (unit_two * gain_two.astype(jnp.float32)).astype(jnp.bfloat16)
    logits = jnp.dot(normed_two, router_w, preferred_element_type=jnp.float32)
    router_probs = jax.nn.softmax(logits, axis=-1)
    choose = (routes == jnp.arange(experts, dtype=jnp.int32)[None, :]).astype(jnp.float32)
    gate_prob = jnp.sum(router_probs * choose, axis=-1)
    earlier = jnp.cumsum(choose, axis=0) - choose
    position = jnp.sum(earlier * choose, axis=-1).astype(jnp.int32) + routes[:, 0] * capacity
    dispatch = (
        position[:, None] == jnp.arange(experts * capacity, dtype=jnp.int32)[None, :]
    ).astype(jnp.bfloat16)
    upstream = cotangent.astype(jnp.float32)
    grad_combined = (gate_prob[:, None] * upstream).astype(jnp.bfloat16)
    slot_shape = (owners, 1, local_experts, capacity, features)

    def to_slots(values):
        return (
            jnp.einsum("lc,ld->cd", dispatch, values, preferred_element_type=jnp.float32)
            .astype(jnp.bfloat16)
            .reshape(slot_shape)
        )

    outgoing = jnp.concatenate([to_slots(normed_two), to_slots(grad_combined)], axis=1)
    both = lax.all_to_all(outgoing, "expert", split_axis=0, concat_axis=0, tiled=True)
    both_all = lax.all_gather(both, "dp", axis=0, tiled=True)
    arrived, grad_arrived = (both[:, 0], both[:, 1])
    rows_all, grads_all = (both_all[:, 0], both_all[:, 1])
    pre_act = jnp.einsum("secd,edf->secf", arrived, w_in, preferred_element_type=jnp.float32)
    hidden_act, gelu_pull = jax.vjp(gelu_tanh, pre_act)
    produced = jnp.einsum(
        "secf,efd->secd",
        hidden_act.astype(jnp.bfloat16),
        w_out,
        preferred_element_type=jnp.float32,
    ).astype(jnp.bfloat16)
    grad_hidden = jnp.einsum(
        "secd,efd->secf", grad_arrived, w_out, preferred_element_type=jnp.float32
    )
    grad_pre = gelu_pull(grad_hidden)[0].astype(jnp.bfloat16)
    grad_rows = jnp.einsum(
        "secf,edf->secd", grad_pre, w_in, preferred_element_type=jnp.float32
    ).astype(jnp.bfloat16)
    results = jnp.stack([produced, grad_rows], axis=1)
    returned = lax.all_to_all(results, "expert", split_axis=0, concat_axis=0, tiled=True)

    def from_slots(values):
        return jnp.einsum(
            "lc,cd->ld",
            dispatch,
            values.reshape(experts * capacity, features),
            preferred_element_type=jnp.float32,
        )

    combined = from_slots(returned[:, 0])
    grad_normed_expert = from_slots(returned[:, 1])
    output = residual + gate_prob[:, None] * combined
    grad_gate = jnp.sum(upstream * combined, axis=-1)
    grad_logits = (grad_gate * gate_prob)[:, None] * (choose - router_probs)
    grad_router = jnp.dot(normed_two.astype(jnp.float32).T, grad_logits, precision=highest)
    grad_normed_router = jnp.dot(grad_logits, router_w.astype(jnp.float32).T, precision=highest)
    hidden_part = w_in.shape[2] // dp_size
    first_hidden = lax.axis_index("dp") * hidden_part
    in_part = lax.dynamic_slice_in_dim(w_in, first_hidden, hidden_part, axis=2)
    out_part = lax.dynamic_slice_in_dim(w_out, first_hidden, hidden_part, axis=1)
    pre_all = jnp.einsum("secd,edf->secf", rows_all, in_part, preferred_element_type=jnp.float32)
    act_all, pull_all = jax.vjp(gelu_tanh, pre_all)
    grad_hidden_all = jnp.einsum(
        "secd,efd->secf", grads_all, out_part, preferred_element_type=jnp.float32
    )
    pre_part = pull_all(grad_hidden_all)[0].astype(jnp.bfloat16)
    act_part = act_all.astype(jnp.bfloat16)
    grad_first_w = jnp.einsum(
        "secd,secf->edf", rows_all, pre_part, preferred_element_type=jnp.float32
    )
    grad_second_w = jnp.einsum(
        "secf,secd->efd", act_part, grads_all, preferred_element_type=jnp.float32
    )
    grad_normed_two = grad_normed_router + grad_normed_expert
    grad_gain_two, grad_through = norm_back(
        grad_normed_two, unit_two, scale_two, gain_two.astype(jnp.float32)
    )
    grad_residual = upstream + grad_through
    grad_attn = grad_residual.astype(jnp.bfloat16)
    grad_output_w = jnp.einsum("ld,le->de", attended, grad_attn, preferred_element_type=jnp.float32)
    grad_attended = (
        jnp.einsum("le,de->ld", grad_attn, output_w, preferred_element_type=jnp.float32)
        .astype(jnp.bfloat16)
        .reshape(length, num_heads, head_size)
    )
    attn_probs = jnp.exp(scores_of() - log_total)
    grad_value = jnp.einsum(
        "hqk,qhe->khe",
        attn_probs.astype(jnp.bfloat16),
        grad_attended,
        preferred_element_type=jnp.float32,
    ).astype(jnp.bfloat16)
    grad_probs = jnp.einsum(
        "qhe,khe->hqk", grad_attended, valued, preferred_element_type=jnp.float32
    )
    grad_scores = attn_probs * (
        grad_probs - jnp.sum(grad_probs * attn_probs, axis=-1, keepdims=True)
    )
    bias_value, bias_pull = jax.vjp(
        lambda table_bias: bias_table(table_bias, bucket_table), rel_bias
    )
    grad_rel = bias_pull(grad_scores)[0]
    scores_low = grad_scores.astype(jnp.bfloat16)
    grad_query = (
        jnp.einsum("hqk,khe->qhe", scores_low, keyed, preferred_element_type=jnp.float32)
        .astype(jnp.bfloat16)
        .reshape(length, features)
    )
    grad_key = (
        jnp.einsum("hqk,qhe->khe", scores_low, query, preferred_element_type=jnp.float32)
        .astype(jnp.bfloat16)
        .reshape(length, features)
    )
    grad_value = grad_value.reshape(length, features)
    grad_query_w = jnp.einsum("ld,le->de", normed, grad_query, preferred_element_type=jnp.float32)
    grad_key_w = jnp.einsum("ld,le->de", normed, grad_key, preferred_element_type=jnp.float32)
    grad_value_w = jnp.einsum("ld,le->de", normed, grad_value, preferred_element_type=jnp.float32)
    grad_normed_one = jnp.einsum(
        "le,de->ld", grad_query, query_w, preferred_element_type=jnp.float32
    )
    grad_normed_one = grad_normed_one + jnp.einsum(
        "le,de->ld", grad_key, key_w, preferred_element_type=jnp.float32
    )
    grad_normed_one = grad_normed_one + jnp.einsum(
        "le,de->ld", grad_value, value_w, preferred_element_type=jnp.float32
    )
    grad_gain_one, grad_inner = norm_back(
        grad_normed_one, unit_one, scale_one, gain_one.astype(jnp.float32)
    )
    grad_inputs = grad_residual + grad_inner
    extra_grads = jnp.concatenate(
        [grad_router, grad_gain_one[:, None], grad_gain_two[:, None]], axis=1
    )
    send_one = widen(
        jnp.concatenate([grad_query_w, grad_key_w, extra_grads], axis=1).astype(jnp.bfloat16),
        width_one,
    )
    send_two = widen(
        jnp.concatenate([grad_value_w, grad_output_w], axis=1).astype(jnp.bfloat16), width_two
    )
    entries = grad_rel.size
    small_rows = -(-entries // 1024) * 8
    small = jnp.pad(grad_rel.reshape(-1), (0, small_rows * 128 - entries))
    sum_one, sum_two, small_sum = scatter_sums(
        (
            send_one.reshape((-1,) + block_shape(rows, width_one)),
            send_two.reshape((-1,) + block_shape(rows, width_two)),
        ),
        small.reshape(small_rows, 128),
        dp_size,
        owners,
    )
    sum_one = sum_one.reshape(rows, width_one)
    sum_two = sum_two.reshape(rows, width_two)
    grad_rel_all = small_sum.reshape(-1)[:entries].reshape(grad_rel.shape)
    first_extra = 2 * features
    return (
        output.astype(jnp.bfloat16),
        grad_inputs.astype(jnp.bfloat16),
        sum_one[:, first_extra + experts],
        sum_one[:, :features],
        sum_one[:, features : 2 * features],
        sum_two[:, :features],
        sum_two[:, features : 2 * features],
        grad_rel_all,
        sum_one[:, first_extra + experts + 1],
        sum_one[:, first_extra : first_extra + experts],
        grad_first_w,
        grad_second_w,
    )


def solution(mesh):
    return jax.shard_map(
        per_device,
        mesh=mesh,
        in_specs=(
            P(("dp", "expert"), None),
            P(("dp", "expert"), None),
            P(("dp", "expert"), None),
            P(),
            P(("dp", "expert")),
            P(("dp", "expert"), None),
            P(("dp", "expert"), None),
            P(("dp", "expert"), None),
            P(("dp", "expert"), None),
            P(),
            P(("dp", "expert")),
            P(("dp", "expert"), None),
            P("expert", None, None),
            P("expert", None, None),
            P(("dp", "expert"), None),
        ),
        out_specs=(
            P(("dp", "expert"), None),
            P(("dp", "expert"), None),
            P(("dp", "expert")),
            P(("dp", "expert"), None),
            P(("dp", "expert"), None),
            P(("dp", "expert"), None),
            P(("dp", "expert"), None),
            P(),
            P(("dp", "expert")),
            P(("dp", "expert"), None),
            P("expert", None, "dp"),
            P("expert", "dp", None),
        ),
        check_vma=False,
    )
```

```python
import functools

import jax
import jax.numpy as jnp
from jax import lax
from jax.experimental import pallas as pl
from jax.experimental.pallas import tpu as pltpu
from jax.sharding import PartitionSpec as P

epsilon = 1e-06
highest = lax.Precision.HIGHEST


def gelu_tanh(values):
    return jax.nn.gelu(values, approximate=True)


def offset_onehot(bucket_table, buckets):
    return (
        bucket_table[:, None] == jnp.arange(buckets, dtype=jnp.int32)[None, :]
    ).astype(jnp.float32)


def doubling(count):
    return [2**step for step in range(count.bit_length() - 1)]


def exchange_orders(dp_size, expert_size):
    x_size = dp_size // 2
    y_size = min(x_size, expert_size)
    z_size = expert_size // y_size
    along_y = doubling(y_size)
    along_z = [y_size * step for step in doubling(z_size)]
    cores = [expert_size]
    along_x = [2 * expert_size * step for step in doubling(x_size)]
    return (along_z + along_y + along_x + cores, along_z + along_x + along_y + cores)


def signed(me, weight):
    return weight * (1 - 2 * ((me // weight) % 2))


def member(me, order, slot):
    other = me
    for step, weight in enumerate(order):
        other = other + ((slot // 2**step) % 2) * signed(me, weight)
    return other


def device_of(index, expert_size):
    return (index // expert_size, index % expert_size)


def meet(me, weights, expert_size):
    barrier = pltpu.get_barrier_semaphore()
    for weight in weights:
        pl.semaphore_signal(
            barrier,
            inc=1,
            device_id=device_of(me + signed(me, weight), expert_size),
            device_id_type=pl.DeviceIdType.MESH,
        )
    pl.semaphore_wait(barrier, len(weights))


def send(me, weight, expert_size, source, target, send_sem, recv_sem):
    copy = pltpu.make_async_remote_copy(
        src_ref=source,
        dst_ref=target,
        send_sem=send_sem,
        recv_sem=recv_sem,
        device_id=device_of(me + signed(me, weight), expert_size),
        device_id_type=pl.DeviceIdType.MESH,
    )
    copy.start()
    return copy


def gather_kernel(orders, expert_size, *refs):
    shards, outs, held, sems = refs[:2], refs[2:4], refs[4:6], refs[6:]
    send_sem, recv_sem = sems
    me = lax.axis_index("dp") * expert_size + lax.axis_index("expert")
    stages = len(orders[0])
    for shard, buffer in zip(shards, held):
        buffer[0] = shard[...]
    meet(me, orders[0], expert_size)
    copies = [[], []]
    for stage in range(stages):
        size = 2**stage
        for part in range(2):
            if stage:
                copies[part][-1].wait_recv()
            copies[part].append(
                send(
                    me,
                    orders[part][stage],
                    expert_size,
                    held[part].at[pl.ds(0, size)],
                    held[part].at[pl.ds(size, size)],
                    send_sem.at[part, stage],
                    recv_sem.at[part, stage],
                )
            )

    def place(part, first, last):
        def body(slot, carry):
            outs[part][member(me, orders[part], slot)] = held[part][slot]
            return carry

        lax.fori_loop(first, last, body, 0)

    half = 2 ** (stages - 1)
    for part in range(2):
        place(part, 0, half)
    for part in range(2):
        copies[part][-1].wait_recv()
        place(part, half, 2 * half)
    for part in range(2):
        for copy in copies[part]:
            copy.wait_send()


def gather_shards(shards, dp_size, expert_size):
    count = dp_size * expert_size
    orders = exchange_orders(dp_size, expert_size)
    stages = len(orders[0])
    shapes = [(count,) + shard.shape for shard in shards]
    vmem = pl.BlockSpec(memory_space=pltpu.VMEM)
    return pl.pallas_call(
        functools.partial(gather_kernel, orders, expert_size),
        out_shape=[jax.ShapeDtypeStruct(shape, jnp.bfloat16) for shape in shapes],
        in_specs=[vmem] * 2,
        out_specs=[vmem] * 2,
        scratch_shapes=[pltpu.VMEM(shape, jnp.bfloat16) for shape in shapes]
        + [pltpu.SemaphoreType.DMA((2, stages)), pltpu.SemaphoreType.DMA((2, stages))],
        compiler_params=pltpu.CompilerParams(
            collective_id=0, has_side_effects=True, vmem_limit_bytes=40 * 2**20
        ),
    )(*shards)


def scatter_kernel(orders, expert_size, *refs):
    grads, small, outs, small_out = refs[:2], refs[2], refs[3:5], refs[5]
    held, landed, small_held, small_landed = refs[6:8], refs[8:10], refs[10], refs[11]
    send_sem, recv_sem = refs[12:]
    me = lax.axis_index("dp") * expert_size + lax.axis_index("expert")
    stages = len(orders[0])
    count = 2**stages
    half = count // 2

    def fill(part, first, last):
        def body(slot, carry):
            held[part][slot] = grads[part][member(me, orders[part], slot)]
            return carry

        lax.fori_loop(first, last, body, 0)

    def start(part, stage):
        size = 2**stage
        return send(
            me,
            orders[part][stage],
            expert_size,
            held[part].at[pl.ds(size, size)],
            landed[part].at[pl.ds(size, size)],
            send_sem.at[part, stage],
            recv_sem.at[part, stage],
        )

    def start_small(stage):
        return send(
            me,
            orders[0][stage],
            expert_size,
            small_held.at[stage],
            small_landed.at[stage],
            send_sem.at[2, stage],
            recv_sem.at[2, stage],
        )

    small_held[stages - 1] = small[...]
    fill(0, half, count)
    meet(me, orders[0], expert_size)
    started = [start(0, stages - 1)]
    fill(1, half, count)
    started.append(start(1, stages - 1))
    small_copy = start_small(stages - 1)
    fill(0, 0, half)
    fill(1, 0, half)
    sent = []
    current = list(started)
    for stage in reversed(range(stages)):
        size = 2**stage
        for part in range(2):
            current[part].wait_recv()
            sent.append(current[part])
            if stage:

                def body(slot, carry):
                    held[part][slot] = (
                        held[part][slot].astype(jnp.float32)
                        + landed[part][slot + size].astype(jnp.float32)
                    ).astype(jnp.bfloat16)
                    return carry

                lax.fori_loop(size // 2, size, body, 0)
                current[part] = start(part, stage - 1)
                lax.fori_loop(0, size // 2, body, 0)
            else:
                outs[part][...] = held[part][0].astype(jnp.float32) + landed[part][1].astype(
                    jnp.float32
                )
        small_copy.wait_recv()
        sent.append(small_copy)
        total = small_held[stage] + small_landed[stage]
        if stage:
            small_held[stage - 1] = total
            small_copy = start_small(stage - 1)
        else:
            small_out[...] = total
    for copy in sent:
        copy.wait_send()


def scatter_sums(grads, small, dp_size, expert_size):
    orders = exchange_orders(dp_size, expert_size)
    stages = len(orders[0])
    shapes = [grad.shape for grad in grads]
    vmem = pl.BlockSpec(memory_space=pltpu.VMEM)
    buffers = [pltpu.VMEM(shape, jnp.bfloat16) for shape in shapes]
    small_buffer = pltpu.VMEM((stages,) + small.shape, jnp.float32)
    return pl.pallas_call(
        functools.partial(scatter_kernel, orders, expert_size),
        out_shape=[jax.ShapeDtypeStruct(shape[1:], jnp.float32) for shape in shapes]
        + [jax.ShapeDtypeStruct(small.shape, jnp.float32)],
        in_specs=[vmem] * 3,
        out_specs=[vmem] * 3,
        scratch_shapes=buffers
        + buffers
        + [small_buffer] * 2
        + [pltpu.SemaphoreType.DMA((3, stages)), pltpu.SemaphoreType.DMA((3, stages))],
        compiler_params=pltpu.CompilerParams(
            collective_id=1, has_side_effects=True, vmem_limit_bytes=40 * 2**20
        ),
    )(*grads, small)


def padded_width(width, rows):
    unit = 128 if rows % 8 == 0 else 2048
    return -(-width // unit) * unit


def block_shape(rows, width):
    return (rows, width) if rows % 8 == 0 else (16, rows * width // 16)


def widen(array, width):
    return jnp.pad(array, ((0, 0), (0, width - array.shape[1])))


def contract(left, right, dims, precision=None):
    return lax.dot_general(
        left,
        right,
        (((dims[0],), (dims[1],)), ((), ())),
        precision=precision,
        preferred_element_type=jnp.float32,
    )


def unit_rows(values):
    scale = lax.rsqrt(jnp.mean(values * values, axis=-1, keepdims=True) + epsilon)
    return (scale, values * scale)


def gain_rows(one_ref, features, experts):
    turned = one_ref[:, 2 * features : 2 * features + 128].astype(jnp.float32).T
    return (turned[experts : experts + 1], turned[experts + 1 : experts + 2])


def forward_kernel(
    experts,
    capacity,
    heads,
    tokens,
    segment_col,
    segment_row,
    routes,
    table,
    one_ref,
    two_ref,
    cotangent,
    normed_ref,
    query_ref,
    keyed_ref,
    valued_ref,
    probs_ref,
    attended_ref,
    residual_ref,
    normed_two_ref,
    router_ref,
    dispatch_ref,
    slots_ref,
):
    length, features = tokens.shape
    size = features // heads
    inputs = tokens[...].astype(jnp.float32)
    gain_one, gain_two = gain_rows(one_ref, features, experts)
    normed = (unit_rows(inputs)[1] * gain_one).astype(jnp.bfloat16)
    normed_ref[...] = normed
    query_ref[...] = contract(normed, one_ref[:, :features], (1, 0)).astype(jnp.bfloat16)
    keyed_ref[...] = contract(normed, one_ref[:, features : 2 * features], (1, 0)).astype(
        jnp.bfloat16
    )
    valued_ref[...] = contract(normed, two_ref[:, :features], (1, 0)).astype(jnp.bfloat16)
    same_doc = segment_col[...] == segment_row[...]
    for head in range(heads):
        span = slice(head * size, (head + 1) * size)
        spread = jnp.broadcast_to(table[head : head + 1, :], (length, 2 * length))
        bias = pltpu.roll(spread, length + 1, 1, stride=1, stride_axis=0)[:, :length]
        scores = contract(query_ref[:, span], keyed_ref[:, span], (1, 1)) + bias
        scores = jnp.where(same_doc, scores, -1e30)
        powers = jnp.exp(scores - jnp.max(scores, axis=-1, keepdims=True))
        probs = powers / jnp.sum(powers, axis=-1, keepdims=True)
        probs_ref[head] = probs
        attended_ref[:, span] = contract(
            probs.astype(jnp.bfloat16), valued_ref[:, span], (1, 0)
        ).astype(jnp.bfloat16)
    residual = inputs + contract(attended_ref[...], two_ref[:, features : 2 * features], (1, 0))
    residual_ref[...] = residual
    normed_two = (unit_rows(residual)[1] * gain_two).astype(jnp.bfloat16)
    normed_two_ref[...] = normed_two
    lanes = lax.broadcasted_iota(jnp.int32, (length, 128), 1)
    logits = contract(normed_two, one_ref[:, 2 * features : 2 * features + 128], (1, 0))
    logits = jnp.where(lanes < experts, logits, -1e30)
    powers = jnp.exp(logits - jnp.max(logits, axis=-1, keepdims=True))
    router = powers / jnp.sum(powers, axis=-1, keepdims=True)
    router_ref[...] = router
    choose = (routes[...] == lanes).astype(jnp.float32)
    gate = jnp.sum(router * choose, axis=-1, keepdims=True)
    rows = lax.broadcasted_iota(jnp.int32, (length, length), 0)
    columns = lax.broadcasted_iota(jnp.int32, (length, length), 1)
    below = (columns < rows).astype(jnp.float32).astype(jnp.bfloat16)
    earlier = contract(below, choose.astype(jnp.bfloat16), (1, 0))
    position = jnp.sum(earlier * choose, axis=-1, keepdims=True).astype(jnp.int32)
    position = position + routes[...] * (2 * capacity)
    places = lax.broadcasted_iota(jnp.int32, (length, 2 * experts * capacity), 1)
    token_place = (places == position).astype(jnp.float32)
    grad_place = (places == position + capacity).astype(jnp.float32)
    dispatch = jnp.concatenate([token_place, grad_place], axis=0).astype(jnp.bfloat16)
    dispatch_ref[...] = dispatch
    weighted = (gate * cotangent[...].astype(jnp.float32)).astype(jnp.bfloat16)
    slots_ref[...] = contract(
        dispatch, jnp.concatenate([normed_two, weighted], axis=0), (0, 0)
    ).astype(jnp.bfloat16)


def backward_kernel(
    experts,
    heads,
    tokens,
    routes,
    one_ref,
    two_ref,
    cotangent,
    normed_ref,
    query_ref,
    keyed_ref,
    valued_ref,
    probs_ref,
    attended_ref,
    residual_ref,
    normed_two_ref,
    router_ref,
    dispatch_ref,
    returned_ref,
    output_ref,
    grad_tokens_ref,
    grad_one_ref,
    grad_two_ref,
    offsets_ref,
    grad_query_ref,
    grad_key_ref,
    grad_value_ref,
):
    length, features = tokens.shape
    size = features // heads
    last = 2 * features
    gain_one, gain_two = gain_rows(one_ref, features, experts)
    scale_one, unit_one = unit_rows(tokens[...].astype(jnp.float32))
    residual = residual_ref[...]
    scale_two, unit_two = unit_rows(residual)
    upstream = cotangent[...].astype(jnp.float32)
    both = contract(dispatch_ref[...], returned_ref[...], (1, 0))
    combined = both[:length]
    lanes = lax.broadcasted_iota(jnp.int32, (length, 128), 1)
    choose = (routes[...] == lanes).astype(jnp.float32)
    router = router_ref[...]
    gate = jnp.sum(router * choose, axis=-1, keepdims=True)
    output_ref[...] = (residual + gate * combined).astype(jnp.bfloat16)
    grad_gate = jnp.sum(upstream * combined, axis=-1, keepdims=True)
    grad_logits = grad_gate * gate * (choose - router)
    router_w = one_ref[:, last : last + 128].astype(jnp.float32)
    grad_normed_two = both[length:] + contract(grad_logits, router_w, (1, 1), highest)
    grad_unit = grad_normed_two * gain_two
    grad_residual = upstream + scale_two * (
        grad_unit - unit_two * jnp.mean(grad_unit * unit_two, axis=-1, keepdims=True)
    )
    grad_attn = grad_residual.astype(jnp.bfloat16)
    grad_two_ref[:, features:last] = contract(attended_ref[...], grad_attn, (0, 0)).astype(
        jnp.bfloat16
    )
    grad_attended = contract(grad_attn, two_ref[:, features:last], (1, 1)).astype(jnp.bfloat16)
    rows = lax.broadcasted_iota(jnp.int32, (length, length), 0)
    columns = lax.broadcasted_iota(jnp.int32, (length, length), 1)
    turn = (rows + columns == length - 1).astype(jnp.float32)
    for head in range(heads):
        span = slice(head * size, (head + 1) * size)
        probs = probs_ref[head]
        grad_head = grad_attended[:, span]
        grad_value_ref[:, span] = contract(probs.astype(jnp.bfloat16), grad_head, (0, 0)).astype(
            jnp.bfloat16
        )
        grad_probs = contract(grad_head, valued_ref[:, span], (1, 1))
        grad_scores = probs * (grad_probs - jnp.sum(grad_probs * probs, axis=-1, keepdims=True))
        turned = contract(turn, grad_scores, (1, 0), highest)
        spread = jnp.concatenate([turned, jnp.zeros_like(turned)], axis=1)
        spread = pltpu.roll(spread, 0, 1, stride=1, stride_axis=0)
        offsets_ref[head : head + 1, :] = jnp.sum(spread, axis=0, keepdims=True)
        scores_low = grad_scores.astype(jnp.bfloat16)
        grad_query_ref[:, span] = contract(scores_low, keyed_ref[:, span], (1, 0)).astype(
            jnp.bfloat16
        )
        grad_key_ref[:, span] = contract(scores_low, query_ref[:, span], (0, 0)).astype(
            jnp.bfloat16
        )
    normed = normed_ref[...]
    grad_query, grad_key, grad_value = (
        grad_query_ref[...],
        grad_key_ref[...],
        grad_value_ref[...],
    )
    grad_one_ref[:, :features] = contract(normed, grad_query, (0, 0)).astype(jnp.bfloat16)
    grad_one_ref[:, features:last] = contract(normed, grad_key, (0, 0)).astype(jnp.bfloat16)
    grad_two_ref[:, :features] = contract(normed, grad_value, (0, 0)).astype(jnp.bfloat16)
    grad_normed = contract(grad_query, one_ref[:, :features], (1, 1))
    grad_normed = grad_normed + contract(grad_key, one_ref[:, features:last], (1, 1))
    grad_normed = grad_normed + contract(grad_value, two_ref[:, :features], (1, 1))
    grad_unit = grad_normed * gain_one
    grad_tokens_ref[...] = (
        grad_residual
        + scale_one
        * (grad_unit - unit_one * jnp.mean(grad_unit * unit_one, axis=-1, keepdims=True))
    ).astype(jnp.bfloat16)
    left = jnp.concatenate(
        [
            normed_two_ref[...].astype(jnp.float32),
            grad_normed * unit_one,
            grad_normed_two * unit_two,
        ],
        axis=0,
    )
    right = jnp.concatenate(
        [
            grad_logits,
            (lanes == experts).astype(jnp.float32),
            (lanes == experts + 1).astype(jnp.float32),
        ],
        axis=0,
    )
    grad_one_ref[:, last : last + 128] = contract(left, right, (0, 0), highest).astype(
        jnp.bfloat16
    )
    if grad_one_ref.shape[1] > last + 128:
        rest = grad_one_ref.shape[1] - last - 128
        grad_one_ref[:, last + 128 :] = jnp.zeros((features, rest), jnp.bfloat16)
    if grad_two_ref.shape[1] > last:
        rest = grad_two_ref.shape[1] - last
        grad_two_ref[:, last:] = jnp.zeros((features, rest), jnp.bfloat16)


def local_call(kernel, inputs, outputs, scratch=(), flops=0):
    vmem = pl.BlockSpec(memory_space=pltpu.VMEM)
    return pl.pallas_call(
        kernel,
        out_shape=[jax.ShapeDtypeStruct(shape, dtype) for shape, dtype in outputs],
        in_specs=[vmem] * len(inputs),
        out_specs=[vmem] * len(outputs),
        scratch_shapes=list(scratch),
        compiler_params=pltpu.CompilerParams(vmem_limit_bytes=50 * 2**20),
        cost_estimate=pl.CostEstimate(
            flops=flops, bytes_accessed=12 * 10**6, transcendentals=200000
        ),
    )(*inputs)


def per_device(
    tokens,
    segment_ids,
    routes,
    bucket_table,
    gain_attn,
    w_query,
    w_key,
    w_value,
    w_output,
    rel_bias,
    gain_ffn,
    w_router,
    w_in,
    w_out,
    cotangent,
):
    length, features = tokens.shape
    num_heads = rel_bias.shape[1]
    head_size = features // num_heads
    local_experts = w_in.shape[0]
    owners = lax.axis_size("expert")
    experts = local_experts * owners
    capacity = 5 * length // (4 * experts)
    dp_size = lax.axis_size("dp")
    rows = w_query.shape[0]
    extras = experts + 2
    width_one = padded_width(2 * features + extras, rows)
    width_two = padded_width(2 * features, rows)
    shard_one = widen(
        jnp.concatenate(
            [w_query, w_key, w_router, gain_attn[:, None], gain_ffn[:, None]], axis=1
        ),
        width_one,
    )
    shard_two = widen(jnp.concatenate([w_value, w_output], axis=1), width_two)
    whole_one, whole_two = gather_shards(
        (
            shard_one.reshape(block_shape(rows, width_one)),
            shard_two.reshape(block_shape(rows, width_two)),
        ),
        dp_size,
        owners,
    )
    whole_one = whole_one.reshape(features, width_one)
    whole_two = whole_two.reshape(features, width_two)
    onehot = offset_onehot(bucket_table, rel_bias.shape[0])
    table = jnp.pad(jnp.dot(onehot, rel_bias, precision=highest).T, ((0, 0), (0, 1)))
    low, full = jnp.bfloat16, jnp.float32
    dense_flops = 2 * length * features * features
    saved = local_call(
        functools.partial(forward_kernel, experts, capacity, num_heads),
        (
            tokens,
            segment_ids.reshape(length, 1),
            segment_ids,
            routes,
            table,
            whole_one,
            whole_two,
            cotangent,
        ),
        [
            ((length, features), low),
            ((length, features), low),
            ((length, features), low),
            ((length, features), low),
            ((num_heads, length, length), full),
            ((length, features), low),
            ((length, features), full),
            ((length, features), low),
            ((length, 128), full),
            ((2 * length, 2 * experts * capacity), low),
            ((2 * experts * capacity, features), low),
        ],
        flops=5 * dense_flops,
    )
    outgoing = saved[-1].reshape(owners, local_experts, 2 * capacity, features)
    both = lax.all_to_all(outgoing, "expert", split_axis=0, concat_axis=0, tiled=True)
    both_all = lax.all_gather(both, "dp", axis=0, tiled=True)
    arrived, grad_arrived = (both[:, :, :capacity], both[:, :, capacity:])
    rows_all, grads_all = (both_all[:, :, :capacity], both_all[:, :, capacity:])
    pre_act = jnp.einsum("secd,edf->secf", arrived, w_in, preferred_element_type=jnp.float32)
    hidden_act, gelu_pull = jax.vjp(gelu_tanh, pre_act)
    produced = jnp.einsum(
        "secf,efd->secd",
        hidden_act.astype(jnp.bfloat16),
        w_out,
        preferred_element_type=jnp.float32,
    ).astype(jnp.bfloat16)
    grad_hidden = jnp.einsum(
        "secd,efd->secf", grad_arrived, w_out, preferred_element_type=jnp.float32
    )
    grad_pre = gelu_pull(grad_hidden)[0].astype(jnp.bfloat16)
    grad_rows = jnp.einsum(
        "secf,edf->secd", grad_pre, w_in, preferred_element_type=jnp.float32
    ).astype(jnp.bfloat16)
    results = jnp.concatenate([produced, grad_rows], axis=2)
    returned = lax.all_to_all(results, "expert", split_axis=0, concat_axis=0, tiled=True)

    output, grad_inputs, send_one, send_two, grad_offsets = local_call(
        functools.partial(backward_kernel, experts, num_heads),
        (
            tokens,
            routes,
            whole_one,
            whole_two,
            cotangent,
            *saved[:-1],
            returned.reshape(2 * experts * capacity, features),
        ),
        [
            ((length, features), low),
            ((length, features), low),
            ((features, width_one), low),
            ((features, width_two), low),
            ((num_heads, 2 * length), full),
        ],
        scratch=[pltpu.VMEM((length, features), low)] * 3,
        flops=10 * dense_flops,
    )
    grad_rel = jnp.dot(onehot.T, grad_offsets[:, :-1].T, precision=highest)
    hidden_part = w_in.shape[2] // dp_size
    first_hidden = lax.axis_index("dp") * hidden_part
    in_part = lax.dynamic_slice_in_dim(w_in, first_hidden, hidden_part, axis=2)
    out_part = lax.dynamic_slice_in_dim(w_out, first_hidden, hidden_part, axis=1)
    pre_all = jnp.einsum("secd,edf->secf", rows_all, in_part, preferred_element_type=jnp.float32)
    act_all, pull_all = jax.vjp(gelu_tanh, pre_all)
    grad_hidden_all = jnp.einsum(
        "secd,efd->secf", grads_all, out_part, preferred_element_type=jnp.float32
    )
    pre_part = pull_all(grad_hidden_all)[0].astype(jnp.bfloat16)
    act_part = act_all.astype(jnp.bfloat16)
    grad_first_w = jnp.einsum(
        "secd,secf->edf", rows_all, pre_part, preferred_element_type=jnp.float32
    )
    grad_second_w = jnp.einsum(
        "secf,secd->efd", act_part, grads_all, preferred_element_type=jnp.float32
    )
    entries = grad_rel.size
    small_rows = -(-entries // 1024) * 8
    small = jnp.pad(grad_rel.reshape(-1), (0, small_rows * 128 - entries))
    sum_one, sum_two, small_sum = scatter_sums(
        (
            send_one.reshape((-1,) + block_shape(rows, width_one)),
            send_two.reshape((-1,) + block_shape(rows, width_two)),
        ),
        small.reshape(small_rows, 128),
        dp_size,
        owners,
    )
    sum_one = sum_one.reshape(rows, width_one)
    sum_two = sum_two.reshape(rows, width_two)
    grad_rel_all = small_sum.reshape(-1)[:entries].reshape(grad_rel.shape)
    first_extra = 2 * features
    return (
        output,
        grad_inputs,
        sum_one[:, first_extra + experts],
        sum_one[:, :features],
        sum_one[:, features : 2 * features],
        sum_two[:, :features],
        sum_two[:, features : 2 * features],
        grad_rel_all,
        sum_one[:, first_extra + experts + 1],
        sum_one[:, first_extra : first_extra + experts],
        grad_first_w,
        grad_second_w,
    )


def solution(mesh):
    return jax.shard_map(
        per_device,
        mesh=mesh,
        in_specs=(
            P(("dp", "expert"), None),
            P(("dp", "expert"), None),
            P(("dp", "expert"), None),
            P(),
            P(("dp", "expert")),
            P(("dp", "expert"), None),
            P(("dp", "expert"), None),
            P(("dp", "expert"), None),
            P(("dp", "expert"), None),
            P(),
            P(("dp", "expert")),
            P(("dp", "expert"), None),
            P("expert", None, None),
            P("expert", None, None),
            P(("dp", "expert"), None),
        ),
        out_specs=(
            P(("dp", "expert"), None),
            P(("dp", "expert"), None),
            P(("dp", "expert")),
            P(("dp", "expert"), None),
            P(("dp", "expert"), None),
            P(("dp", "expert"), None),
            P(("dp", "expert"), None),
            P(),
            P(("dp", "expert")),
            P(("dp", "expert"), None),
            P("expert", None, "dp"),
            P("expert", "dp", None),
        ),
        check_vma=False,
    )
```

```python
import functools

import jax
import jax.numpy as jnp
from jax import lax
from jax.experimental import pallas as pl
from jax.experimental.pallas import tpu as pltpu
from jax.sharding import PartitionSpec as P

epsilon = 1e-06
highest = lax.Precision.HIGHEST


def gelu_tanh(values):
    return jax.nn.gelu(values, approximate=True)


def offset_onehot(bucket_table, buckets):
    return (
        bucket_table[:, None] == jnp.arange(buckets, dtype=jnp.int32)[None, :]
    ).astype(jnp.float32)


def doubling(count):
    return [2**step for step in range(count.bit_length() - 1)]


def exchange_orders(dp_size, expert_size):
    x_size = dp_size // 2
    y_size = min(x_size, expert_size)
    z_size = expert_size // y_size
    along_y = doubling(y_size)
    along_z = [y_size * step for step in doubling(z_size)]
    cores = [expert_size]
    along_x = [2 * expert_size * step for step in doubling(x_size)]
    return (
        along_z + along_y + along_x + cores,
        along_z + along_x + along_y + cores,
        along_y + along_x + along_z + cores,
        along_x + along_y + along_z + cores,
    )


def column_parts(widths):
    cuts = [max(128, width * 4 // 5 // 128 * 128) for width in widths]
    return (
        (0, 0, cuts[0]),
        (1, 0, cuts[1]),
        (0, cuts[0], widths[0]),
        (1, cuts[1], widths[1]),
    )


def signed(me, weight):
    return weight * (1 - 2 * ((me // weight) % 2))


def member(me, order, slot):
    other = me
    for step, weight in enumerate(order):
        other = other + ((slot // 2**step) % 2) * signed(me, weight)
    return other


def device_of(index, expert_size):
    return (index // expert_size, index % expert_size)


def meet(me, weights, expert_size):
    barrier = pltpu.get_barrier_semaphore()
    for weight in weights:
        pl.semaphore_signal(
            barrier,
            inc=1,
            device_id=device_of(me + signed(me, weight), expert_size),
            device_id_type=pl.DeviceIdType.MESH,
        )
    pl.semaphore_wait(barrier, len(weights))


def send(me, weight, expert_size, source, target, send_sem, recv_sem):
    copy = pltpu.make_async_remote_copy(
        src_ref=source,
        dst_ref=target,
        send_sem=send_sem,
        recv_sem=recv_sem,
        device_id=device_of(me + signed(me, weight), expert_size),
        device_id_type=pl.DeviceIdType.MESH,
    )
    copy.start()
    return copy


def gather_kernel(orders, parts, expert_size, *refs):
    shards, outs, held = refs[:2], refs[2:4], refs[4:-2]
    send_sem, recv_sem = refs[-2:]
    me = lax.axis_index("dp") * expert_size + lax.axis_index("expert")
    stages = len(orders[0])
    count = len(parts)
    for (array, first, last), buffer in zip(parts, held):
        buffer[0] = shards[array][:, first:last]
    meet(me, orders[0], expert_size)
    copies = [[] for _ in parts]
    for stage in range(stages):
        size = 2**stage
        for part in range(count):
            if stage:
                copies[part][-1].wait_recv()
            copies[part].append(
                send(
                    me,
                    orders[part][stage],
                    expert_size,
                    held[part].at[pl.ds(0, size)],
                    held[part].at[pl.ds(size, size)],
                    send_sem.at[part, stage],
                    recv_sem.at[part, stage],
                )
            )

    def place(part, begin, end):
        array, first, last = parts[part]

        def body(slot, carry):
            outs[array][member(me, orders[part], slot), :, first:last] = held[part][slot]
            return carry

        lax.fori_loop(begin, end, body, 0)

    half = 2 ** (stages - 1)
    for part in range(count):
        place(part, 0, half)
    for part in range(count):
        copies[part][-1].wait_recv()
        place(part, half, 2 * half)
    for part in range(count):
        for copy in copies[part]:
            copy.wait_send()


def gather_shards(shards, dp_size, expert_size):
    count = dp_size * expert_size
    orders = exchange_orders(dp_size, expert_size)
    stages = len(orders[0])
    shapes = [(count,) + shard.shape for shard in shards]
    parts = column_parts([shard.shape[1] for shard in shards])
    vmem = pl.BlockSpec(memory_space=pltpu.VMEM)
    return pl.pallas_call(
        functools.partial(gather_kernel, orders, parts, expert_size),
        out_shape=[jax.ShapeDtypeStruct(shape, jnp.bfloat16) for shape in shapes],
        in_specs=[vmem] * 2,
        out_specs=[vmem] * 2,
        scratch_shapes=[
            pltpu.VMEM((count, shards[array].shape[0], last - first), jnp.bfloat16)
            for array, first, last in parts
        ]
        + [pltpu.SemaphoreType.DMA((len(parts), stages))] * 2,
        compiler_params=pltpu.CompilerParams(
            collective_id=0, has_side_effects=True, vmem_limit_bytes=40 * 2**20
        ),
    )(*shards)


def scatter_kernel(orders, parts, expert_size, *refs):
    total_parts = len(parts)
    grads, small, outs, small_out = refs[:2], refs[2], refs[3:5], refs[5]
    held, landed = refs[6 : 6 + total_parts], refs[6 + total_parts : 6 + 2 * total_parts]
    small_held, small_landed, send_sem, recv_sem = refs[6 + 2 * total_parts :]
    me = lax.axis_index("dp") * expert_size + lax.axis_index("expert")
    stages = len(orders[0])
    count = 2**stages
    half = count // 2

    def fill(part, begin, end):
        array, first, last = parts[part]

        def body(slot, carry):
            held[part][slot] = grads[array][member(me, orders[part], slot), :, first:last]
            return carry

        lax.fori_loop(begin, end, body, 0)

    def start(part, stage):
        size = 2**stage
        return send(
            me,
            orders[part][stage],
            expert_size,
            held[part].at[pl.ds(size, size)],
            landed[part].at[pl.ds(size, size)],
            send_sem.at[part, stage],
            recv_sem.at[part, stage],
        )

    def start_small(stage):
        return send(
            me,
            orders[0][stage],
            expert_size,
            small_held.at[stage],
            small_landed.at[stage],
            send_sem.at[total_parts, stage],
            recv_sem.at[total_parts, stage],
        )

    small_held[stages - 1] = small[...]
    fill(0, half, count)
    meet(me, orders[0], expert_size)
    current = [start(0, stages - 1)]
    for part in range(1, total_parts):
        fill(part, half, count)
        current.append(start(part, stages - 1))
    small_copy = start_small(stages - 1)
    for part in range(total_parts):
        fill(part, 0, half)
    sent = []
    for stage in reversed(range(stages)):
        size = 2**stage
        for part in range(total_parts):
            current[part].wait_recv()
            sent.append(current[part])
            if stage:

                def body(slot, carry):
                    held[part][slot] = (
                        held[part][slot].astype(jnp.float32)
                        + landed[part][slot + size].astype(jnp.float32)
                    ).astype(jnp.bfloat16)
                    return carry

                lax.fori_loop(size // 2, size, body, 0)
                current[part] = start(part, stage - 1)
                lax.fori_loop(0, size // 2, body, 0)
            else:
                array, first, last = parts[part]
                outs[array][:, first:last] = held[part][0].astype(jnp.float32) + landed[part][
                    1
                ].astype(jnp.float32)
        small_copy.wait_recv()
        sent.append(small_copy)
        total = small_held[stage] + small_landed[stage]
        if stage:
            small_held[stage - 1] = total
            small_copy = start_small(stage - 1)
        else:
            small_out[...] = total
    for copy in sent:
        copy.wait_send()


def scatter_sums(grads, small, dp_size, expert_size):
    orders = exchange_orders(dp_size, expert_size)
    stages = len(orders[0])
    shapes = [grad.shape for grad in grads]
    parts = column_parts([shape[2] for shape in shapes])
    vmem = pl.BlockSpec(memory_space=pltpu.VMEM)
    buffers = [
        pltpu.VMEM(shapes[array][:2] + (last - first,), jnp.bfloat16)
        for array, first, last in parts
    ]
    small_buffer = pltpu.VMEM((stages,) + small.shape, jnp.float32)
    return pl.pallas_call(
        functools.partial(scatter_kernel, orders, parts, expert_size),
        out_shape=[jax.ShapeDtypeStruct(shape[1:], jnp.float32) for shape in shapes]
        + [jax.ShapeDtypeStruct(small.shape, jnp.float32)],
        in_specs=[vmem] * 3,
        out_specs=[vmem] * 3,
        scratch_shapes=buffers
        + buffers
        + [small_buffer] * 2
        + [pltpu.SemaphoreType.DMA((len(parts) + 1, stages))] * 2,
        compiler_params=pltpu.CompilerParams(
            collective_id=1, has_side_effects=True, vmem_limit_bytes=40 * 2**20
        ),
    )(*grads, small)


def padded_width(width, rows):
    unit = 128 if rows % 8 == 0 else 2048
    return -(-width // unit) * unit


def block_shape(rows, width):
    return (rows, width) if rows % 8 == 0 else (16, rows * width // 16)


def widen(array, width):
    return jnp.pad(array, ((0, 0), (0, width - array.shape[1])))


def contract(left, right, dims, precision=None):
    return lax.dot_general(
        left,
        right,
        (((dims[0],), (dims[1],)), ((), ())),
        precision=precision,
        preferred_element_type=jnp.float32,
    )


def unit_rows(values):
    scale = lax.rsqrt(jnp.mean(values * values, axis=-1, keepdims=True) + epsilon)
    return (scale, values * scale)


def gain_rows(one_ref, features, experts):
    turned = one_ref[:, 2 * features : 2 * features + 128].astype(jnp.float32).T
    return (turned[experts : experts + 1], turned[experts + 1 : experts + 2])


def forward_kernel(
    experts,
    capacity,
    heads,
    tokens,
    segment_col,
    segment_row,
    routes,
    table,
    one_ref,
    two_ref,
    cotangent,
    normed_ref,
    query_ref,
    keyed_ref,
    valued_ref,
    probs_ref,
    attended_ref,
    residual_ref,
    normed_two_ref,
    router_ref,
    dispatch_ref,
    slots_ref,
):
    length, features = tokens.shape
    size = features // heads
    inputs = tokens[...].astype(jnp.float32)
    gain_one, gain_two = gain_rows(one_ref, features, experts)
    normed = (unit_rows(inputs)[1] * gain_one).astype(jnp.bfloat16)
    normed_ref[...] = normed
    query_ref[...] = contract(normed, one_ref[:, :features], (1, 0)).astype(jnp.bfloat16)
    keyed_ref[...] = contract(normed, one_ref[:, features : 2 * features], (1, 0)).astype(
        jnp.bfloat16
    )
    valued_ref[...] = contract(normed, two_ref[:, :features], (1, 0)).astype(jnp.bfloat16)
    same_doc = segment_col[...] == segment_row[...]
    for head in range(heads):
        span = slice(head * size, (head + 1) * size)
        spread = jnp.broadcast_to(table[head : head + 1, :], (length, 2 * length))
        bias = pltpu.roll(spread, length + 1, 1, stride=1, stride_axis=0)[:, :length]
        scores = contract(query_ref[:, span], keyed_ref[:, span], (1, 1)) + bias
        scores = jnp.where(same_doc, scores, -1e30)
        powers = jnp.exp(scores - jnp.max(scores, axis=-1, keepdims=True))
        probs = powers / jnp.sum(powers, axis=-1, keepdims=True)
        probs_ref[head] = probs
        attended_ref[:, span] = contract(
            probs.astype(jnp.bfloat16), valued_ref[:, span], (1, 0)
        ).astype(jnp.bfloat16)
    residual = inputs + contract(attended_ref[...], two_ref[:, features : 2 * features], (1, 0))
    residual_ref[...] = residual
    normed_two = (unit_rows(residual)[1] * gain_two).astype(jnp.bfloat16)
    normed_two_ref[...] = normed_two
    lanes = lax.broadcasted_iota(jnp.int32, (length, 128), 1)
    logits = contract(normed_two, one_ref[:, 2 * features : 2 * features + 128], (1, 0))
    logits = jnp.where(lanes < experts, logits, -1e30)
    powers = jnp.exp(logits - jnp.max(logits, axis=-1, keepdims=True))
    router = powers / jnp.sum(powers, axis=-1, keepdims=True)
    router_ref[...] = router
    choose = (routes[...] == lanes).astype(jnp.float32)
    gate = jnp.sum(router * choose, axis=-1, keepdims=True)
    rows = lax.broadcasted_iota(jnp.int32, (length, length), 0)
    columns = lax.broadcasted_iota(jnp.int32, (length, length), 1)
    below = (columns < rows).astype(jnp.float32).astype(jnp.bfloat16)
    earlier = contract(below, choose.astype(jnp.bfloat16), (1, 0))
    position = jnp.sum(earlier * choose, axis=-1, keepdims=True).astype(jnp.int32)
    position = position + routes[...] * (2 * capacity)
    places = lax.broadcasted_iota(jnp.int32, (length, 2 * experts * capacity), 1)
    token_place = (places == position).astype(jnp.float32)
    grad_place = (places == position + capacity).astype(jnp.float32)
    dispatch = jnp.concatenate([token_place, grad_place], axis=0).astype(jnp.bfloat16)
    dispatch_ref[...] = dispatch
    weighted = (gate * cotangent[...].astype(jnp.float32)).astype(jnp.bfloat16)
    slots_ref[...] = contract(
        dispatch, jnp.concatenate([normed_two, weighted], axis=0), (0, 0)
    ).astype(jnp.bfloat16)


def backward_kernel(
    experts,
    heads,
    tokens,
    routes,
    one_ref,
    two_ref,
    cotangent,
    normed_ref,
    query_ref,
    keyed_ref,
    valued_ref,
    probs_ref,
    attended_ref,
    residual_ref,
    normed_two_ref,
    router_ref,
    dispatch_ref,
    returned_ref,
    output_ref,
    grad_tokens_ref,
    grad_one_ref,
    grad_two_ref,
    offsets_ref,
    grad_query_ref,
    grad_key_ref,
    grad_value_ref,
):
    length, features = tokens.shape
    size = features // heads
    last = 2 * features
    gain_one, gain_two = gain_rows(one_ref, features, experts)
    scale_one, unit_one = unit_rows(tokens[...].astype(jnp.float32))
    residual = residual_ref[...]
    scale_two, unit_two = unit_rows(residual)
    upstream = cotangent[...].astype(jnp.float32)
    both = contract(dispatch_ref[...], returned_ref[...], (1, 0))
    combined = both[:length]
    lanes = lax.broadcasted_iota(jnp.int32, (length, 128), 1)
    choose = (routes[...] == lanes).astype(jnp.float32)
    router = router_ref[...]
    gate = jnp.sum(router * choose, axis=-1, keepdims=True)
    output_ref[...] = (residual + gate * combined).astype(jnp.bfloat16)
    grad_gate = jnp.sum(upstream * combined, axis=-1, keepdims=True)
    grad_logits = grad_gate * gate * (choose - router)
    router_w = one_ref[:, last : last + 128].astype(jnp.float32)
    grad_normed_two = both[length:] + contract(grad_logits, router_w, (1, 1), highest)
    grad_unit = grad_normed_two * gain_two
    grad_residual = upstream + scale_two * (
        grad_unit - unit_two * jnp.mean(grad_unit * unit_two, axis=-1, keepdims=True)
    )
    grad_attn = grad_residual.astype(jnp.bfloat16)
    grad_two_ref[:, features:last] = contract(attended_ref[...], grad_attn, (0, 0)).astype(
        jnp.bfloat16
    )
    grad_attended = contract(grad_attn, two_ref[:, features:last], (1, 1)).astype(jnp.bfloat16)
    rows = lax.broadcasted_iota(jnp.int32, (length, length), 0)
    columns = lax.broadcasted_iota(jnp.int32, (length, length), 1)
    turn = (rows + columns == length - 1).astype(jnp.float32)
    for head in range(heads):
        span = slice(head * size, (head + 1) * size)
        probs = probs_ref[head]
        grad_head = grad_attended[:, span]
        grad_value_ref[:, span] = contract(probs.astype(jnp.bfloat16), grad_head, (0, 0)).astype(
            jnp.bfloat16
        )
        grad_probs = contract(grad_head, valued_ref[:, span], (1, 1))
        grad_scores = probs * (grad_probs - jnp.sum(grad_probs * probs, axis=-1, keepdims=True))
        turned = contract(turn, grad_scores, (1, 0), highest)
        spread = jnp.concatenate([turned, jnp.zeros_like(turned)], axis=1)
        spread = pltpu.roll(spread, 0, 1, stride=1, stride_axis=0)
        offsets_ref[head : head + 1, :] = jnp.sum(spread, axis=0, keepdims=True)
        scores_low = grad_scores.astype(jnp.bfloat16)
        grad_query_ref[:, span] = contract(scores_low, keyed_ref[:, span], (1, 0)).astype(
            jnp.bfloat16
        )
        grad_key_ref[:, span] = contract(scores_low, query_ref[:, span], (0, 0)).astype(
            jnp.bfloat16
        )
    normed = normed_ref[...]
    grad_query, grad_key, grad_value = (
        grad_query_ref[...],
        grad_key_ref[...],
        grad_value_ref[...],
    )
    grad_one_ref[:, :features] = contract(normed, grad_query, (0, 0)).astype(jnp.bfloat16)
    grad_one_ref[:, features:last] = contract(normed, grad_key, (0, 0)).astype(jnp.bfloat16)
    grad_two_ref[:, :features] = contract(normed, grad_value, (0, 0)).astype(jnp.bfloat16)
    grad_normed = contract(grad_query, one_ref[:, :features], (1, 1))
    grad_normed = grad_normed + contract(grad_key, one_ref[:, features:last], (1, 1))
    grad_normed = grad_normed + contract(grad_value, two_ref[:, :features], (1, 1))
    grad_unit = grad_normed * gain_one
    grad_tokens_ref[...] = (
        grad_residual
        + scale_one
        * (grad_unit - unit_one * jnp.mean(grad_unit * unit_one, axis=-1, keepdims=True))
    ).astype(jnp.bfloat16)
    left = jnp.concatenate(
        [
            normed_two_ref[...].astype(jnp.float32),
            grad_normed * unit_one,
            grad_normed_two * unit_two,
        ],
        axis=0,
    )
    right = jnp.concatenate(
        [
            grad_logits,
            (lanes == experts).astype(jnp.float32),
            (lanes == experts + 1).astype(jnp.float32),
        ],
        axis=0,
    )
    grad_one_ref[:, last : last + 128] = contract(left, right, (0, 0), highest).astype(
        jnp.bfloat16
    )
    if grad_one_ref.shape[1] > last + 128:
        rest = grad_one_ref.shape[1] - last - 128
        grad_one_ref[:, last + 128 :] = jnp.zeros((features, rest), jnp.bfloat16)
    if grad_two_ref.shape[1] > last:
        rest = grad_two_ref.shape[1] - last
        grad_two_ref[:, last:] = jnp.zeros((features, rest), jnp.bfloat16)


def local_call(kernel, inputs, outputs, scratch=(), flops=0):
    vmem = pl.BlockSpec(memory_space=pltpu.VMEM)
    return pl.pallas_call(
        kernel,
        out_shape=[jax.ShapeDtypeStruct(shape, dtype) for shape, dtype in outputs],
        in_specs=[vmem] * len(inputs),
        out_specs=[vmem] * len(outputs),
        scratch_shapes=list(scratch),
        compiler_params=pltpu.CompilerParams(vmem_limit_bytes=50 * 2**20),
        cost_estimate=pl.CostEstimate(
            flops=flops, bytes_accessed=12 * 10**6, transcendentals=200000
        ),
    )(*inputs)


def per_device(
    tokens,
    segment_ids,
    routes,
    bucket_table,
    gain_attn,
    w_query,
    w_key,
    w_value,
    w_output,
    rel_bias,
    gain_ffn,
    w_router,
    w_in,
    w_out,
    cotangent,
):
    length, features = tokens.shape
    num_heads = rel_bias.shape[1]
    head_size = features // num_heads
    local_experts = w_in.shape[0]
    owners = lax.axis_size("expert")
    experts = local_experts * owners
    capacity = 5 * length // (4 * experts)
    dp_size = lax.axis_size("dp")
    rows = w_query.shape[0]
    extras = experts + 2
    width_one = padded_width(2 * features + extras, rows)
    width_two = padded_width(2 * features, rows)
    shard_one = widen(
        jnp.concatenate(
            [w_query, w_key, w_router, gain_attn[:, None], gain_ffn[:, None]], axis=1
        ),
        width_one,
    )
    shard_two = widen(jnp.concatenate([w_value, w_output], axis=1), width_two)
    whole_one, whole_two = gather_shards(
        (
            shard_one.reshape(block_shape(rows, width_one)),
            shard_two.reshape(block_shape(rows, width_two)),
        ),
        dp_size,
        owners,
    )
    whole_one = whole_one.reshape(features, width_one)
    whole_two = whole_two.reshape(features, width_two)
    onehot = offset_onehot(bucket_table, rel_bias.shape[0])
    table = jnp.pad(jnp.dot(onehot, rel_bias, precision=highest).T, ((0, 0), (0, 1)))
    low, full = jnp.bfloat16, jnp.float32
    dense_flops = 2 * length * features * features
    saved = local_call(
        functools.partial(forward_kernel, experts, capacity, num_heads),
        (
            tokens,
            segment_ids.reshape(length, 1),
            segment_ids,
            routes,
            table,
            whole_one,
            whole_two,
            cotangent,
        ),
        [
            ((length, features), low),
            ((length, features), low),
            ((length, features), low),
            ((length, features), low),
            ((num_heads, length, length), full),
            ((length, features), low),
            ((length, features), full),
            ((length, features), low),
            ((length, 128), full),
            ((2 * length, 2 * experts * capacity), low),
            ((2 * experts * capacity, features), low),
        ],
        flops=5 * dense_flops,
    )
    outgoing = saved[-1].reshape(owners, local_experts, 2 * capacity, features)
    both = lax.all_to_all(outgoing, "expert", split_axis=0, concat_axis=0, tiled=True)
    both_all = lax.all_gather(both, "dp", axis=0, tiled=True)
    arrived, grad_arrived = (both[:, :, :capacity], both[:, :, capacity:])
    rows_all, grads_all = (both_all[:, :, :capacity], both_all[:, :, capacity:])
    pre_act = jnp.einsum("secd,edf->secf", arrived, w_in, preferred_element_type=jnp.float32)
    hidden_act, gelu_pull = jax.vjp(gelu_tanh, pre_act)
    produced = jnp.einsum(
        "secf,efd->secd",
        hidden_act.astype(jnp.bfloat16),
        w_out,
        preferred_element_type=jnp.float32,
    ).astype(jnp.bfloat16)
    grad_hidden = jnp.einsum(
        "secd,efd->secf", grad_arrived, w_out, preferred_element_type=jnp.float32
    )
    grad_pre = gelu_pull(grad_hidden)[0].astype(jnp.bfloat16)
    grad_rows = jnp.einsum(
        "secf,edf->secd", grad_pre, w_in, preferred_element_type=jnp.float32
    ).astype(jnp.bfloat16)
    results = jnp.concatenate([produced, grad_rows], axis=2)
    returned = lax.all_to_all(results, "expert", split_axis=0, concat_axis=0, tiled=True)

    hidden_part = w_in.shape[2] // dp_size
    first_hidden = lax.axis_index("dp") * hidden_part
    in_part = lax.dynamic_slice_in_dim(w_in, first_hidden, hidden_part, axis=2)
    out_part = lax.dynamic_slice_in_dim(w_out, first_hidden, hidden_part, axis=1)
    pre_all = jnp.einsum("secd,edf->secf", rows_all, in_part, preferred_element_type=jnp.float32)
    act_all, pull_all = jax.vjp(gelu_tanh, pre_all)
    grad_hidden_all = jnp.einsum(
        "secd,efd->secf", grads_all, out_part, preferred_element_type=jnp.float32
    )
    pre_part = pull_all(grad_hidden_all)[0].astype(jnp.bfloat16)
    act_part = act_all.astype(jnp.bfloat16)
    grad_first_w = jnp.einsum(
        "secd,secf->edf", rows_all, pre_part, preferred_element_type=jnp.float32
    )
    grad_second_w = jnp.einsum(
        "secf,secd->efd", act_part, grads_all, preferred_element_type=jnp.float32
    )
    returned, grad_first_w, grad_second_w = lax.optimization_barrier(
        (returned, grad_first_w, grad_second_w)
    )
    output, grad_inputs, send_one, send_two, grad_offsets = local_call(
        functools.partial(backward_kernel, experts, num_heads),
        (
            tokens,
            routes,
            whole_one,
            whole_two,
            cotangent,
            *saved[:-1],
            returned.reshape(2 * experts * capacity, features),
        ),
        [
            ((length, features), low),
            ((length, features), low),
            ((features, width_one), low),
            ((features, width_two), low),
            ((num_heads, 2 * length), full),
        ],
        scratch=[pltpu.VMEM((length, features), low)] * 3,
        flops=10 * dense_flops,
    )
    grad_rel = jnp.dot(onehot.T, grad_offsets[:, :-1].T, precision=highest)
    entries = grad_rel.size
    small_rows = -(-entries // 1024) * 8
    small = jnp.pad(grad_rel.reshape(-1), (0, small_rows * 128 - entries))
    sum_one, sum_two, small_sum = scatter_sums(
        (
            send_one.reshape((-1,) + block_shape(rows, width_one)),
            send_two.reshape((-1,) + block_shape(rows, width_two)),
        ),
        small.reshape(small_rows, 128),
        dp_size,
        owners,
    )
    sum_one = sum_one.reshape(rows, width_one)
    sum_two = sum_two.reshape(rows, width_two)
    grad_rel_all = small_sum.reshape(-1)[:entries].reshape(grad_rel.shape)
    first_extra = 2 * features
    return (
        output,
        grad_inputs,
        sum_one[:, first_extra + experts],
        sum_one[:, :features],
        sum_one[:, features : 2 * features],
        sum_two[:, :features],
        sum_two[:, features : 2 * features],
        grad_rel_all,
        sum_one[:, first_extra + experts + 1],
        sum_one[:, first_extra : first_extra + experts],
        grad_first_w,
        grad_second_w,
    )


def solution(mesh):
    return jax.shard_map(
        per_device,
        mesh=mesh,
        in_specs=(
            P(("dp", "expert"), None),
            P(("dp", "expert"), None),
            P(("dp", "expert"), None),
            P(),
            P(("dp", "expert")),
            P(("dp", "expert"), None),
            P(("dp", "expert"), None),
            P(("dp", "expert"), None),
            P(("dp", "expert"), None),
            P(),
            P(("dp", "expert")),
            P(("dp", "expert"), None),
            P("expert", None, None),
            P("expert", None, None),
            P(("dp", "expert"), None),
        ),
        out_specs=(
            P(("dp", "expert"), None),
            P(("dp", "expert"), None),
            P(("dp", "expert")),
            P(("dp", "expert"), None),
            P(("dp", "expert"), None),
            P(("dp", "expert"), None),
            P(("dp", "expert"), None),
            P(),
            P(("dp", "expert")),
            P(("dp", "expert"), None),
            P("expert", None, "dp"),
            P("expert", "dp", None),
        ),
        check_vma=False,
    )
```
